32 devices in a mesh: groups: 2 (over y), ha: 8 (over z, x), wa: 2 (over core).
Axes of the slice: x: 2, y: 2, z: 4, core: 2. Of those that a mesh axis runs over, the one named last changes fastest.
Arguments:
- frames_in: float32 [12, 32, 96, 256], P(None, ('groups', 'ha'), None, 'wa'), parts along dimension 1, may hold values from -6 to 6
- clip_frames: int32 [16], P('groups'), parts along dimension 0, may hold values from 2 to 12, as said below
- conv_weight: float32 [4, 3, 3, 3, 96, 96], replicated, may hold values from -0.125 to 0.125
- conv_bias: float32 [4, 96], replicated, may hold values from -3 to 3
- norm_gain: float32 [4, 96], replicated, may hold values from 0.1 to 1.9
Outputs:
- frames_out: float32 [12, 32, 96, 256], P(None, ('groups', 'ha'), None, 'wa'), parts along dimension 1
The draws below stay inside these ranges and needn't reach their ends.
There are 2 independent parts, one for each index of `groups`. The reference program is written for one: setup_inputs(seed, part) draws one part's arguments, and reference() takes and returns one part's arrays. A program takes and returns all parts, laid end to end along the dimension named above; an argument that names none is the same for every part. Nothing has to cross between parts.
Inputs may be any that keep to these rules, and one draw needn't show every extreme that they name: `clip_frames`: the 4 entries of one slab (indices s * 4 + 4 // 2 onward, modulo 8) are equal; some slab holds 12 frames.
All inputs are finite; a program needn't handle non-finite values.
Results may differ from the reference program's by a relative error of at most 0.0001.
Values sent between devices are 32-bit elements; how exact they have to be, the bound alone decides.
A program may use at most 128 MiB of HBM per device.

```python
import jax
import jax.numpy as jnp
from jax import lax

CH = 96
ROWS = 2
FMAX = 12
SLAB_DEVS = 4
BLOCKS = 2
CONVS = 4
SLABS = 2
HEIGHT = 16
WIDTH = 256


def draw_clip_frames(key, part):
    half = SLABS // 2
    key_a, key_b, key_c, key_d, key_e, key_f = jax.random.split(jax.random.fold_in(key, 11), 6)
    heavy = jax.random.randint(key_a, (half,), 2, FMAX + 1)
    light = jnp.minimum(jax.random.randint(key_b, (half,), 2, FMAX + 1), jax.random.randint(key_c, (half,), 2, FMAX + 1))
    light = jnp.minimum(light, jax.random.randint(key_d, (half,), 2, FMAX + 1))
    flipped = jax.random.randint(key_e, (half,), 0, 2)
    first_half = jnp.where(flipped == 1, heavy, light)
    second_half = jnp.where(flipped == 1, light, heavy)
    slab_counts = jnp.concatenate([first_half, second_half])
    chosen = jax.random.randint(key_f, (), 0, half)
    flip_chosen = jnp.sum(jnp.where(jnp.arange(half, dtype=jnp.int32) == chosen, flipped, 0))
    target = jnp.where(flip_chosen == 1, chosen, chosen + half)
    slab_counts = jnp.where(jnp.arange(SLABS, dtype=jnp.int32) == target, FMAX, slab_counts)
    per_device = jnp.repeat(slab_counts, SLAB_DEVS)
    return jnp.roll(per_device, SLAB_DEVS // 2).astype(jnp.int32)


def shard_levels(own_key, dims, shards, least, high):
    factor_of, own = 1.0, jax.random.fold_in(own_key, 6)
    for dim, parts in shards:
        steps = jnp.exp(jax.random.uniform(jax.random.fold_in(own, dim), (parts,), jnp.float32, least / len(shards), high / len(shards)))
        factor_of = factor_of * jnp.repeat(steps, dims[dim] // parts).reshape([-1 if axis == dim else 1 for axis in range(len(dims))])
    return factor_of


def gaussian(own_key, shape, scale, most, pieces=(), kind=jnp.bfloat16):
    level = shard_levels(own_key, shape, pieces, -0.22, 0.18) if pieces else 1.0
    result = jax.random.normal(own_key, shape, jnp.float32) * scale * level
    return jnp.minimum(jnp.maximum(result, -most), most).astype(kind)


def setup_inputs(seed: int = 0, part: int = 0) -> dict:
    splits = jax.random.split(jax.random.key(seed), 6)
    own_keys = jax.random.split(jax.random.fold_in(splits[5], part), 6)
    return {
        "frames_in": gaussian(own_keys[0], (FMAX, HEIGHT, CH, WIDTH), 1.0, 6.0, ((1, 8), (3, 2)), jnp.float32),
        "clip_frames": draw_clip_frames(jax.random.fold_in(jax.random.fold_in(splits[5], part), 71), part),
        "conv_weight": gaussian(splits[2], (CONVS, 3, 3, 3, CH, CH), (27 * CH) ** -0.5, 0.125, (), jnp.float32),
        "conv_bias": gaussian(splits[3], (CONVS, CH), 0.5, 3.0, (), jnp.float32),
        "norm_gain": jnp.clip(1.0 + 0.18 * jax.random.normal(splits[4], (CONVS, CH), jnp.float32), 0.1, 1.9),
    }


EPS = 1e-06

def activate(field, gain):
    scale = lax.rsqrt(lax.optimization_barrier(jnp.mean(field * field, axis=-2, keepdims=True)) + EPS)
    return jax.nn.silu(field * scale * gain[:, None])

def convolve(field, weight, bias):
    frames, slabs, length, chans, width = field.shape
    padded = jnp.pad(field, ((2, 0), (0, 0), (1, 1), (0, 0), (1, 1)))
    total = jnp.zeros((frames, slabs, length, weight.shape[3], width), jnp.float32) + bias[:, None]
    for tap_t in range(3):
        for tap_y in range(3):
            for tap_x in range(3):
                piece = padded[tap_t:tap_t + frames, :, tap_y:tap_y + length, :, tap_x:tap_x + width]
                total = total + jnp.einsum('fslcw,dc->fsldw', piece, weight[tap_t, tap_y, tap_x], precision=lax.Precision.HIGHEST)
    return total

def reference(frames_in, clip_frames, conv_weight, conv_bias, norm_gain):
    frames, height, chans, width = frames_in.shape
    slab_rows = height // SLABS
    offset_rows = SLAB_DEVS // 2 * ROWS
    field = jnp.roll(frames_in, -offset_rows, axis=1).reshape(frames, SLABS, slab_rows, chans, width)
    for block in range(BLOCKS):
        first = 2 * block
        middle = convolve(activate(field, norm_gain[first]), conv_weight[first], conv_bias[first])
        field = field + convolve(activate(middle, norm_gain[first + 1]), conv_weight[first + 1], conv_bias[first + 1])
    field = jnp.roll(field.reshape(frames, height, chans, width), offset_rows, axis=1)
    row_counts = jnp.repeat(clip_frames.astype(jnp.int32), ROWS)
    times = jnp.arange(frames, dtype=jnp.int32)
    live = times[:, None] < row_counts[None, :]
    return jnp.where(live[:, :, None, None], field, jnp.zeros_like(field))
```

```python
import jax
import jax.numpy as jnp
from jax import lax
from jax.sharding import PartitionSpec as P

SPAN = 4
SLAB_DEVS = 4
BLOCKS = 2


EPS = 1e-06


def extended(cells, sides, width):
    for axis, dim in sides:
        count = lax.axis_size(axis)
        head = lax.slice_in_dim(cells, 0, width, axis=dim)
        tail = lax.slice_in_dim(cells, cells.shape[dim] - width, cells.shape[dim], axis=dim)
        cells = jnp.concatenate(
            [
                lax.ppermute(tail, axis, [(i, (i + 1) % count) for i in range(count)]),
                cells,
                lax.ppermute(head, axis, [((i + 1) % count, i) for i in range(count)]),
            ],
            axis=dim,
        )
    return cells


def activate(field, gain):
    scale = lax.rsqrt(jnp.mean(field * field, axis=-2, keepdims=True) + EPS)
    return jax.nn.silu(field * scale * gain[:, None])


def convolve(padded, weight, bias):
    frames = padded.shape[0] - 2
    length = padded.shape[1] - 2
    width = padded.shape[3] - 2
    total = jnp.zeros((frames, length, weight.shape[3], width), jnp.float32) + bias[:, None]
    chans = padded.shape[2]
    columns = jnp.concatenate(
        [
            padded[:, tap_y : tap_y + length, :, tap_x : tap_x + width]
            for tap_y in range(3)
            for tap_x in range(3)
        ],
        axis=2,
    )
    for tap_t in range(3):
        kernel = jnp.moveaxis(weight[tap_t].reshape(9, -1, chans), 0, 1).reshape(-1, 9 * chans)
        total = total + jnp.einsum(
            "frcw,dc->frdw",
            columns[tap_t : tap_t + frames],
            kernel,
            precision=lax.Precision.HIGH,
        )
    return total


def inside(count, offset, base, limit):
    where_at = base + jnp.arange(count, dtype=jnp.int32) - offset
    return (where_at >= 0) & (where_at < limit)


def per_device(frames_in, clip_frames, conv_weight, conv_bias, norm_gain):
    frames, rows, chans, cols = frames_in.shape
    ha_size = lax.axis_size("ha")
    ha_index = lax.axis_index("ha")
    wa_index = lax.axis_index("wa")
    image_cols = lax.axis_size("wa") * cols
    slab_rows = SLAB_DEVS * rows
    row_base = jnp.mod(ha_index - SLAB_DEVS // 2, SLAB_DEVS) * rows
    col_base = wa_index * cols
    spans = frames // SPAN
    slots = jnp.arange(ha_size, dtype=jnp.int32)
    mine = jnp.sum(jnp.where(slots == ha_index, clip_frames, 0))
    mine_spans = (mine + SPAN - 1) // SPAN
    empty = jnp.zeros((SPAN, rows, chans, cols), jnp.float32)

    def conv_layer(field, weight, bias):
        wide = extended(field, (("ha", 1), ("wa", 3)), 1)
        keep_rows = inside(rows + 2, 1, row_base, slab_rows)
        keep_cols = inside(cols + 2, 1, col_base, image_cols)
        keep = keep_rows[None, :, None, None] & keep_cols[None, None, None, :]
        wide = jnp.where(keep, wide, 0.0)
        wide = jnp.pad(wide, ((2, 0), (0, 0), (0, 0), (0, 0)))
        results = []
        for span in range(spans):
            piece = wide[span * SPAN : span * SPAN + SPAN + 2]
            results.append(
                lax.cond(
                    span < mine_spans, lambda p: convolve(p, weight, bias), lambda p: empty, piece
                )
            )
        return jnp.concatenate(results, axis=0)

    field = frames_in
    for block in range(BLOCKS):
        first = 2 * block
        middle = conv_layer(activate(field, norm_gain[first]), conv_weight[first], conv_bias[first])
        field = field + conv_layer(
            activate(middle, norm_gain[first + 1]), conv_weight[first + 1], conv_bias[first + 1]
        )
    live = jnp.arange(frames, dtype=jnp.int32) < mine
    return jnp.where(live[:, None, None, None], field, 0.0)


def solution(mesh):
    placed = (P(None, ("groups", "ha"), None, "wa"), P("groups"), P(), P(), P())
    return jax.shard_map(
        per_device,
        mesh=mesh,
        in_specs=placed,
        out_specs=P(None, ("groups", "ha"), None, "wa"),
        check_vma=False,
    )
```

```python
import jax
import jax.numpy as jnp
from jax import lax
from jax.sharding import PartitionSpec as P

SPAN = 4
SLAB_DEVS = 4
BLOCKS = 2


EPS = 1e-06


def extended(cells, sides, width):
    for axis, dim in sides:
        count = lax.axis_size(axis)
        head = lax.slice_in_dim(cells, 0, width, axis=dim)
        tail = lax.slice_in_dim(cells, cells.shape[dim] - width, cells.shape[dim], axis=dim)
        cells = jnp.concatenate(
            [
                lax.ppermute(tail, axis, [(i, (i + 1) % count) for i in range(count)]),
                cells,
                lax.ppermute(head, axis, [((i + 1) % count, i) for i in range(count)]),
            ],
            axis=dim,
        )
    return cells


def activate(field, gain):
    scale = lax.rsqrt(jnp.mean(field * field, axis=-2, keepdims=True) + EPS)
    return jax.nn.silu(field * scale * gain[:, None])


def convolve(padded, weight, bias):
    frames = padded.shape[0] - 2
    length = padded.shape[1] - 2
    width = padded.shape[3] - 2
    total = jnp.zeros((frames, length, weight.shape[3], width), jnp.float32) + bias[:, None]
    for tap_t in range(3):
        for tap_y in range(3):
            for tap_x in range(3):
                piece = padded[
                    tap_t : tap_t + frames, tap_y : tap_y + length, :, tap_x : tap_x + width
                ]
                total = total + jnp.einsum(
                    "frcw,dc->frdw",
                    piece,
                    weight[tap_t, tap_y, tap_x],
                    precision=lax.Precision.HIGH,
                )
    return total


def inside(count, offset, base, limit):
    where_at = base + jnp.arange(count, dtype=jnp.int32) - offset
    return (where_at >= 0) & (where_at < limit)


def per_device(frames_in, clip_frames, conv_weight, conv_bias, norm_gain):
    frames, rows, chans, cols = frames_in.shape
    ha_size = lax.axis_size("ha")
    ha_index = lax.axis_index("ha")
    wa_index = lax.axis_index("wa")
    image_cols = lax.axis_size("wa") * cols
    slab_rows = SLAB_DEVS * rows
    row_base = jnp.mod(ha_index - SLAB_DEVS // 2, SLAB_DEVS) * rows
    col_base = wa_index * cols
    spans = frames // SPAN
    slots = jnp.arange(ha_size, dtype=jnp.int32)
    mine = jnp.sum(jnp.where(slots == ha_index, clip_frames, 0))
    mine_spans = (mine + SPAN - 1) // SPAN
    empty = jnp.zeros((SPAN, rows, chans, cols), jnp.float32)

    def conv_layer(field, weight, bias):
        wide = extended(field, (("ha", 1), ("wa", 3)), 1)
        keep_rows = inside(rows + 2, 1, row_base, slab_rows)
        keep_cols = inside(cols + 2, 1, col_base, image_cols)
        keep = keep_rows[None, :, None, None] & keep_cols[None, None, None, :]
        wide = jnp.where(keep, wide, 0.0)
        wide = jnp.pad(wide, ((2, 0), (0, 0), (0, 0), (0, 0)))
        results = []
        for span in range(spans):
            piece = wide[span * SPAN : span * SPAN + SPAN + 2]
            results.append(
                lax.cond(
                    span < mine_spans, lambda p: convolve(p, weight, bias), lambda p: empty, piece
                )
            )
        return jnp.concatenate(results, axis=0)

    field = frames_in
    for block in range(BLOCKS):
        first = 2 * block
        middle = conv_layer(activate(field, norm_gain[first]), conv_weight[first], conv_bias[first])
        field = field + conv_layer(
            activate(middle, norm_gain[first + 1]), conv_weight[first + 1], conv_bias[first + 1]
        )
    live = jnp.arange(frames, dtype=jnp.int32) < mine
    return jnp.where(live[:, None, None, None], field, 0.0)


def solution(mesh):
    placed = (P(None, ("groups", "ha"), None, "wa"), P("groups"), P(), P(), P())
    return jax.shard_map(
        per_device,
        mesh=mesh,
        in_specs=placed,
        out_specs=P(None, ("groups", "ha"), None, "wa"),
        check_vma=False,
    )
```
